128 devices in a mesh: dp: 16 (over y, z_hi, core), mp: 8 (over z_lo, x).
Axes of the slice: x: 4, y: 4, z: 4 (z_hi: 2, z_lo: 2; z = z_hi * 2 + z_lo), core: 2. Of those that a mesh axis runs over, the one named last changes fastest.
Arguments:
- activations: bfloat16 [16384, 4096], P(('dp', 'mp')), may hold values from -6 to 6
- out_grad: bfloat16 [16384, 8192], P('dp', 'mp'), may hold values from -0.046875 to 0.046875
- statistics: float32 [8, 16, 2, 512, 512], P('mp', 'dp'), as said below
- root_blocks: float32 [8, 16, 2, 512, 512], P('mp', 'dp'), as said below
- owner_slots: int32 [8, 16], P('mp'), may hold values from 0 to 15, each once within a row
- stagger_phase: int32 [8], P('mp'), may hold values from 0 to 7
Outputs:
- update: bfloat16 [4096, 8192], P(None, 'mp')
- new_statistics: float32 [8, 16, 2, 512, 512], P('mp', 'dp')
- new_roots: float32 [8, 16, 2, 512, 512], P('mp', 'dp')
The draws below stay inside these ranges and needn't reach their ends.
Inputs may be any that keep to these rules, and one draw needn't show every extreme that they name: `statistics`: each [m, s, side] matrix is symmetric positive definite. `root_blocks`: each [m, s, side] matrix is symmetric positive definite. `owner_slots`: row m gives every block of model shard m its own slot.
All inputs are finite; a program needn't handle non-finite values.
Results may differ from the reference program's by a relative error of at most 0.019.
Values may be sent and summed in bfloat16 or wider, within the bound.
No kernel may reach another device: no remote copies, remote signals or barrier semaphores. Data moves between devices by JAX's collectives and lax.ppermute only.
A program may use at most 128 MiB of HBM per device.

```python
import math
import jax
import jax.numpy as jnp
from jax import lax

FEAT = 4096
QCOLS = 8192
BLOCK = 512
ITERS = 3
TOK_DEV = 1024
TOKENS = 16384
ROW_BLK = 8
COL_BLK = 2
BLK_MP = 16
REFRESH = 2
N_DP = 16
N_MP = 8


def spd_blocks(key, array_shape, off_scale, low_end, high_end):
    block_order = array_shape[-1]
    first_key, second_key, third_key = jax.random.split(key, 3)
    uniform_part = jax.random.uniform(first_key, array_shape, jnp.float32, -1.0, 1.0)
    symmetric = 0.5 * (uniform_part + jnp.swapaxes(uniform_part, -1, -2))
    identity = jnp.eye(block_order, dtype=jnp.float32)
    diagonal = off_scale * (block_order - 1) * jax.random.uniform(second_key, array_shape[:-1], jnp.float32, 1.1, 2.0)
    matrix = off_scale * symmetric * (1.0 - identity) + identity * diagonal[..., None]
    spread_scale = jnp.exp(jax.random.uniform(third_key, array_shape[:-1], jnp.float32, math.log(low_end), math.log(high_end)))
    return matrix * spread_scale[..., :, None] * spread_scale[..., None, :]


def kernel_blocks(key, array_shape, low_end, high_end):
    block_order = array_shape[-1]
    point_key, flip_key, shift_key, scale_key = jax.random.split(key, 4)
    points = jax.random.uniform(point_key, array_shape[:-1] + (3,), jnp.float32, 0.0, 1.0)
    length_scale = (2.0 / block_order) ** (1.0 / 3.0)
    distance = jnp.zeros(array_shape, jnp.float32)
    for which_dim in range(3):
        coordinate = points[..., which_dim]
        distance = distance + jnp.abs(coordinate[..., :, None] - coordinate[..., None, :])
    kernel = jnp.exp(-distance / length_scale)
    sign_flips = jax.random.rademacher(flip_key, array_shape[:-1]).astype(jnp.float32)
    identity = jnp.eye(block_order, dtype=jnp.float32)
    diagonal = jax.random.uniform(shift_key, array_shape[:-1], jnp.float32, 0.3, 0.8)
    matrix = kernel * sign_flips[..., :, None] * sign_flips[..., None, :] + identity * diagonal[..., None]
    spread_scale = jnp.exp(jax.random.uniform(scale_key, array_shape[:-1], jnp.float32, math.log(low_end), math.log(high_end)))
    return matrix * spread_scale[..., :, None] * spread_scale[..., None, :]


def draw_statistics(key, part):
    key = jax.random.fold_in(key, 11)
    array_shape = (N_MP, BLK_MP, 2, BLOCK, BLOCK)
    return spd_blocks(key, array_shape, 0.6 * BLOCK / (BLOCK - 1), 1.0, 1.0)


def draw_root_blocks(key, part):
    key = jax.random.fold_in(key, 12)
    array_shape = (N_MP, BLK_MP, 2, BLOCK, BLOCK)
    return kernel_blocks(key, array_shape, 1.0, 1.0)


def with_ends(values, rng, least, top_value):
    spot = [jax.random.randint(jax.random.fold_in(rng, axis), (), 0, length) for axis, length in enumerate(values.shape)]
    longest = values.shape.index(max(values.shape))
    neighbour = spot[:longest] + [(spot[longest] + 1) % values.shape[longest]] + spot[longest + 1:]
    return values.at[tuple(spot)].set(least).at[tuple(neighbour)].set(top_value)


def steps_of(stream_key, extent, cuts, smallest, top_value):
    gain, own = 1.0, jax.random.fold_in(stream_key, 6)
    for position, blocks in cuts:
        steps = jnp.exp(jax.random.uniform(jax.random.fold_in(own, position), (blocks,), jnp.float32, smallest / len(cuts), top_value / len(cuts)))
        gain = gain * jnp.repeat(steps, extent[position] // blocks).reshape([-1 if axis == position else 1 for axis in range(len(extent))])
    return gain


def centred(rng, extent, spread, reach, shards=(), kind=jnp.bfloat16):
    entries = jax.random.normal(rng, extent, jnp.float32) * spread
    if len(shards) > 0:
        entries = steps_of(rng, extent, shards, -0.22, 0.18) * entries
    return jnp.clip(entries, min=-reach, max=reach).astype(kind)


def setup_inputs(seed: int = 0) -> dict:
    key_of = jax.random.split(jax.random.key(seed), 7)
    activations = centred(key_of[0], (TOKENS, FEAT), 1.0, 6.0, ((0, 128),))
    out_grad = centred(key_of[1], (TOKENS, QCOLS), (1.0 / TOKENS ** 0.5), 0.046875, ((0, 16), (1, 8)))
    statistics = draw_statistics(jax.random.fold_in(key_of[6], 71), 0)
    root_blocks = draw_root_blocks(jax.random.fold_in(key_of[6], 71), 0)
    owner_slots = jax.vmap(lambda own: jax.random.permutation(own, BLK_MP))(jax.random.split(key_of[4], N_MP)).reshape((N_MP, BLK_MP)).astype(jnp.int32)
    stagger_phase = with_ends(jax.random.randint(key_of[5], (N_MP,), 0, 8), jax.random.fold_in(key_of[5], 1), 0, 7).astype(jnp.int32)
    return {"activations": activations, "out_grad": out_grad, "statistics": statistics, "root_blocks": root_blocks, "owner_slots": owner_slots, "stagger_phase": stagger_phase}


def product(left_side, right_side):
    return jnp.dot(left_side, right_side, precision=lax.Precision.HIGHEST, preferred_element_type=jnp.float32)

def inverse_root(matrix):
    identity = jnp.eye(BLOCK, dtype=jnp.float32)
    scaling = 2.5 / jnp.sqrt(jnp.sum(matrix * matrix))
    iterate = identity * jnp.sqrt(jnp.sqrt(scaling))
    coupled = matrix * scaling
    for iteration in range(ITERS):
        factor = (5.0 * identity - coupled) * 0.25
        iterate = product(iterate, factor)
        square = product(factor, factor)
        fourth = product(square, square)
        coupled = product(fourth, coupled)
    return iterate

def reference(activations, out_grad, statistics, root_blocks, owner_slots, stagger_phase):
    tokens_in = activations.reshape(N_DP, TOK_DEV, FEAT)
    grads_out = out_grad.reshape(N_DP, TOK_DEV, QCOLS)

    def accumulate(running, token_pair):
        inputs, outputs = token_pair
        partial_term = jnp.dot(inputs.astype(jnp.float32).T, outputs.astype(jnp.float32), preferred_element_type=jnp.float32)
        rounded = lax.optimization_barrier(partial_term.astype(jnp.bfloat16))
        return (running + rounded.astype(jnp.float32), None)
    full_grad, unused = lax.scan(accumulate, jnp.zeros((FEAT, QCOLS), jnp.float32), (tokens_in, grads_out))
    blocks = full_grad.reshape(ROW_BLK, BLOCK, N_MP, COL_BLK, BLOCK).transpose(2, 0, 3, 1, 4).reshape(N_MP, BLK_MP, BLOCK, BLOCK)
    shard_index = jnp.arange(N_MP, dtype=jnp.int32)[:, None]
    slotted = jnp.zeros_like(blocks).at[shard_index, owner_slots].set(blocks)
    highest = lax.Precision.HIGHEST
    left_gram = jnp.einsum('msij,mskj->msik', slotted, slotted, precision=highest)
    right_gram = jnp.einsum('msji,msjk->msik', slotted, slotted, precision=highest)
    new_statistics = 0.95 * statistics + jnp.stack([left_gram, right_gram], axis=2)
    applied = jnp.einsum('msij,msjk->msik', root_blocks[:, :, 0], slotted, precision=highest)
    applied = jnp.einsum('msij,msjk->msik', applied, root_blocks[:, :, 1], precision=highest)
    ordered = applied[shard_index, owner_slots]
    update = ordered.reshape(N_MP, ROW_BLK, COL_BLK, BLOCK, BLOCK).transpose(1, 3, 0, 2, 4).reshape(FEAT, QCOLS).astype(jnp.bfloat16)
    first_block = (8 - stagger_phase) % 8
    refresh_blocks = first_block[:, None] + 8 * jnp.arange(REFRESH, dtype=jnp.int32)[None, :]
    refresh_slots = jnp.take_along_axis(owner_slots, refresh_blocks, axis=1)
    chosen = new_statistics[shard_index, refresh_slots]
    solved = lax.map(inverse_root, chosen.reshape(-1, BLOCK, BLOCK)).reshape(chosen.shape)
    new_roots = root_blocks.at[shard_index, refresh_slots].set(solved)
    return (update, new_statistics, new_roots)
```

```python
import functools

import jax
import jax.numpy as jnp
from jax import lax
from jax.experimental import pallas as pl
from jax.experimental.pallas import tpu as pltpu
from jax.sharding import PartitionSpec as P

FEAT = 4096
BLOCK = 512
ROW_BLK = 8
COL_BLK = 2
BLOCKS = ROW_BLK * COL_BLK
CHUNKS = (256, 256)
Y, ZH, CORE, ZL, X = 4, 2, 2, 2, 4
N_MP = ZL * X
MIB = 1 << 20


def device_of(y, zh, core, zl, x):
    return ((y * ZH + zh) * CORE + core) * N_MP + zl * X + x


def pairs(move):
    out = []
    for y in range(Y):
        for zh in range(ZH):
            for core in range(CORE):
                for zl in range(ZL):
                    for x in range(X):
                        here = (y, zh, core, zl, x)
                        out.append((device_of(*here), device_of(*move(*here))))
    return out


def way(core):
    return 1 if core == 0 else -1


X_NEAR = pairs(lambda y, zh, c, zl, x: (y, zh, c, zl, (x + way(c)) % X))
X_BACK = pairs(lambda y, zh, c, zl, x: (y, zh, c, zl, (x - way(c)) % X))
Y_NEAR = pairs(lambda y, zh, c, zl, x: ((y + way(c)) % Y, zh, c, zl, x))
Y_BACK = pairs(lambda y, zh, c, zl, x: ((y - way(c)) % Y, zh, c, zl, x))
Y_FAR = pairs(lambda y, zh, c, zl, x: ((y + 2) % Y, zh, c, zl, x))
ZL_SWAP = pairs(lambda y, zh, c, zl, x: (y, zh, c, 1 - zl, x))
ZH_SWAP = pairs(lambda y, zh, c, zl, x: (y, 1 - zh, c, zl, x))
C_SWAP = pairs(lambda y, zh, c, zl, x: (y, zh, 1 - c, zl, x))


def move(value, route):
    return lax.ppermute(value, ("dp", "mp"), route)


def cost(flops, moved):
    return pl.CostEstimate(flops=int(flops), bytes_accessed=int(moved), transcendentals=0)


def params(mib, grid=1):
    return pltpu.CompilerParams(
        vmem_limit_bytes=mib * MIB, dimension_semantics=("arbitrary",) * grid
    )


def mm(a, b, contract):
    return lax.dot_general(a, b, (contract, ((), ())), preferred_element_type=jnp.float32)


def split(value):
    high = value.astype(jnp.bfloat16)
    return high, (value - high.astype(jnp.float32)).astype(jnp.bfloat16)


def mm3(a, b, contract=((1,), (0,))):
    a_high, a_low = a
    b_high, b_low = b
    return (
        mm(a_high, b_high, contract) + mm(a_high, b_low, contract) + mm(a_low, b_high, contract)
    )


def grad_kernel(rows_of, dest_of, *refs):
    pieces = refs[:N_MP]
    og_ref, keep_ref, send_ref, gathered, tiles, sems = refs[N_MP:]
    row = pl.program_id(0)
    part = pieces[0].shape[0]
    for i in range(N_MP):
        gathered[pl.ds(pl.multiple_of(rows_of[i] * part, part), part), :] = pieces[i][...]
    grad = mm(gathered[...], og_ref[...], ((0,), (0,)))
    for col in range(COL_BLK):
        number = row * COL_BLK + col
        dest = dest_of[number]
        tiles[number] = grad[:, col * BLOCK : (col + 1) * BLOCK].astype(jnp.bfloat16)

        @pl.when(dest < BLOCKS // 2)
        def _():
            pltpu.make_async_copy(tiles.at[number], keep_ref.at[dest], sems.at[number]).start()

        @pl.when(dest >= BLOCKS // 2)
        def _():
            pltpu.make_async_copy(
                tiles.at[number], send_ref.at[dest - BLOCKS // 2], sems.at[number]
            ).start()

    @pl.when(row == ROW_BLK - 1)
    def _():
        for number in range(BLOCKS):
            pltpu.make_async_copy(tiles.at[number], keep_ref.at[0], sems.at[number]).wait()


def grad_chunk(pieces, rows_of, dest_of, og, rows):
    part = pieces[0].shape[0]
    tokens, cols = og.shape
    half = jax.ShapeDtypeStruct((BLOCKS // 2, rows, BLOCK), jnp.bfloat16)
    return pl.pallas_call(
        grad_kernel,
        out_shape=(half, half),
        grid_spec=pltpu.PrefetchScalarGridSpec(
            num_scalar_prefetch=2,
            grid=(ROW_BLK,),
            in_specs=[pl.BlockSpec((part, rows), lambda r, *_: (0, r))] * N_MP
            + [pl.BlockSpec((tokens, cols), lambda r, *_: (0, 0))],
            out_specs=[pl.BlockSpec(memory_space=pl.ANY)] * 2,
            scratch_shapes=[
                pltpu.VMEM((tokens, rows), jnp.bfloat16),
                pltpu.VMEM((BLOCKS, rows, BLOCK), jnp.bfloat16),
                pltpu.SemaphoreType.DMA((BLOCKS,)),
            ],
        ),
        compiler_params=params(32),
        cost_estimate=cost(2 * tokens * cols * rows * ROW_BLK, 2 * 5 * MIB),
        name="grad_chunk",
    )(rows_of, dest_of, *pieces, og)


def chip_kernel(_, *refs):
    for d in range(Y):
        total = refs[d][...].astype(jnp.float32) + refs[Y + d][...].astype(jnp.float32)
        refs[2 * Y + d][...] = total.astype(jnp.bfloat16)


def chip_sum(keep, received, groups):
    rows = keep.shape[1]
    block = (1, rows, BLOCK)
    ins = [
        pl.BlockSpec(block, functools.partial(lambda d, j, g: (g[d] * ZH + j, 0, 0), d))
        for d in range(Y)
    ]
    out = jax.ShapeDtypeStruct((ZH, rows, BLOCK), jnp.bfloat16)
    return pl.pallas_call(
        chip_kernel,
        out_shape=(out,) * Y,
        grid_spec=pltpu.PrefetchScalarGridSpec(
            num_scalar_prefetch=1,
            grid=(ZH,),
            in_specs=ins + ins,
            out_specs=[pl.BlockSpec(block, lambda j, g: (j, 0, 0))] * Y,
        ),
        compiler_params=params(16),
        cost_estimate=cost(MIB, keep.size * 6),
        name="chip_sum",
    )(groups, *[keep] * Y, *[received] * Y)


def y_kernel(_, *refs):
    mine = sum(refs[i][0].astype(jnp.float32) for i in range(Y))
    other = sum(refs[Y + i][0].astype(jnp.float32) for i in range(Y))
    refs[2 * Y][...] = mine
    refs[2 * Y + 1][...] = other.astype(jnp.bfloat16)


def y_sum(parts, zh):
    rows = parts[0].shape[1]
    tile = min(rows, 128)
    mine = pl.BlockSpec((1, tile, BLOCK), lambda j, z: (z[0], j, 0))
    other = pl.BlockSpec((1, tile, BLOCK), lambda j, z: (1 - z[0], j, 0))
    out = pl.BlockSpec((tile, BLOCK), lambda j, z: (j, 0))
    return pl.pallas_call(
        y_kernel,
        out_shape=(
            jax.ShapeDtypeStruct((rows, BLOCK), jnp.float32),
            jax.ShapeDtypeStruct((rows, BLOCK), jnp.bfloat16),
        ),
        grid_spec=pltpu.PrefetchScalarGridSpec(
            num_scalar_prefetch=1,
            grid=(rows // tile,),
            in_specs=[mine] * Y + [other] * Y,
            out_specs=[out, out],
        ),
        compiler_params=params(16),
        cost_estimate=cost(MIB, rows * BLOCK * 22),
        name="y_sum",
    )(zh, *parts, *parts)


def apply_kernel(*refs):
    count = len(CHUNKS)
    roots_ref, update_ref, grad_ref = refs[2 * count :]
    at = 0
    for i, rows in enumerate(CHUNKS):
        grad_ref[at : at + rows] = refs[i][...] + refs[count + i][...].astype(jnp.float32)
        at += rows
    grad = split(grad_ref[...])
    right = mm3(grad, split(roots_ref[1]))
    update_ref[...] = mm3(split(roots_ref[0]), split(right)).astype(jnp.bfloat16)


def apply_roots(kept, received, roots):
    whole = pl.BlockSpec(memory_space=pltpu.VMEM)
    return pl.pallas_call(
        apply_kernel,
        out_shape=(
            jax.ShapeDtypeStruct((BLOCK, BLOCK), jnp.bfloat16),
            jax.ShapeDtypeStruct((BLOCK, BLOCK), jnp.float32),
        ),
        in_specs=[whole] * (2 * len(CHUNKS) + 1),
        out_specs=(whole, whole),
        compiler_params=pltpu.CompilerParams(vmem_limit_bytes=24 * MIB),
        cost_estimate=cost(6 * 2 * BLOCK**3, 5 * MIB),
        name="apply_roots",
    )(*kept, *received, roots)


def stats_kernel(grad_ref, stats_ref, out_ref):
    grad = split(grad_ref[...])
    out_ref[0] = 0.95 * stats_ref[0] + mm3(grad, grad, ((1,), (1,)))
    out_ref[1] = 0.95 * stats_ref[1] + mm3(grad, grad, ((0,), (0,)))


def statistics_of(grad, stats):
    whole = pl.BlockSpec(memory_space=pltpu.VMEM)
    return pl.pallas_call(
        stats_kernel,
        out_shape=jax.ShapeDtypeStruct(stats.shape, jnp.float32),
        in_specs=[whole] * 2,
        out_specs=whole,
        compiler_params=pltpu.CompilerParams(vmem_limit_bytes=24 * MIB),
        cost_estimate=cost(6 * 2 * BLOCK**3, 5 * MIB),
        name="statistics",
    )(grad, stats)


def roots_kernel(flag, stats_ref, roots_ref, out_ref):
    @pl.when(flag[0] == 0)
    def _():
        out_ref[...] = roots_ref[...]

    @pl.when(flag[0] != 0)
    def _():
        row = lax.broadcasted_iota(jnp.int32, (BLOCK, BLOCK), 0)
        col = lax.broadcasted_iota(jnp.int32, (BLOCK, BLOCK), 1)
        identity = (row == col).astype(jnp.float32)

        def times(a, b):
            return mm(a.astype(jnp.bfloat16), b.astype(jnp.bfloat16), ((1,), (0,)))

        def powered(coupled):
            rest = times(coupled, coupled) * 0.0625 - 0.625 * coupled
            rest = times(rest, rest) + 3.125 * rest
            return times(rest, coupled) + 2.44140625 * coupled

        for side in range(2):
            matrix = stats_ref[side]
            scaling = 2.5 / jnp.sqrt(jnp.sum(matrix * matrix, keepdims=True))
            first = matrix * scaling
            second = powered(first)
            third = powered(second)
            both = times(first, second) * 0.0625 - 0.3125 * (first + second) + 1.5625 * identity
            found = 1.25 * both - 0.25 * times(both, third)
            out_ref[side] = found * jnp.sqrt(jnp.sqrt(scaling))


def roots_of(flag, stats, roots):
    whole = pl.BlockSpec(memory_space=pltpu.VMEM)
    return pl.pallas_call(
        roots_kernel,
        out_shape=jax.ShapeDtypeStruct(stats.shape, jnp.float32),
        in_specs=[pl.BlockSpec(memory_space=pltpu.SMEM), whole, whole],
        out_specs=whole,
        compiler_params=pltpu.CompilerParams(vmem_limit_bytes=32 * MIB),
        cost_estimate=cost(16 * 2 * BLOCK**3, 6 * MIB),
        name="roots",
    )(flag, stats, roots)


def place_kernel(count, aliased, number_of, *refs):
    blocks = refs[:count]
    out_ref, sems = refs[count + aliased], refs[count + aliased + 1]
    copies = []
    for i in range(count):
        number = number_of[i]
        row = pl.multiple_of(number // COL_BLK * BLOCK, BLOCK)
        col = pl.multiple_of(number % COL_BLK * BLOCK, BLOCK)
        copy = pltpu.make_async_copy(
            blocks[i], out_ref.at[pl.ds(row, BLOCK), pl.ds(col, BLOCK)], sems.at[i]
        )
        copy.start()
        copies.append(copy)
    for copy in copies:
        copy.wait()


def place(blocks, numbers, into, cols):
    count = len(blocks)
    aliased = into is not None
    anywhere = pl.BlockSpec(memory_space=pl.ANY)
    return pl.pallas_call(
        functools.partial(place_kernel, count, int(aliased)),
        out_shape=jax.ShapeDtypeStruct((FEAT, cols), jnp.bfloat16),
        in_specs=[pl.BlockSpec(memory_space=pltpu.SMEM)] + [anywhere] * (count + aliased),
        out_specs=anywhere,
        scratch_shapes=[pltpu.SemaphoreType.DMA((count,))],
        input_output_aliases={count + 1: 0} if aliased else {},
        cost_estimate=cost(0, count * MIB),
        name="place",
    )(jnp.stack(numbers), *blocks, *([into] if aliased else []))


def body(activations, out_grad, statistics, root_blocks, owner_slots, stagger_phase):
    dp, mp = lax.axis_index("dp"), lax.axis_index("mp")
    y, zh, core = dp // (ZH * CORE), dp // CORE % ZH, dp % CORE
    zl, x = mp // X, mp % X
    step = 1 - 2 * core
    slot_of = owner_slots[0]
    numbers = jnp.arange(BLOCKS, dtype=jnp.int32)
    block_at = jnp.sum(jnp.where(slot_of[:, None] == numbers[None, :], numbers[:, None], 0), axis=0)
    dest_of = jnp.where(slot_of % CORE == core, 0, BLOCKS // 2) + slot_of // CORE
    rows_of = []
    for side in (zl, 1 - zl):
        rows_of += [side * X + (x + shift) % X for shift in (0, -step, step, 2)]
    rows_of = jnp.stack(rows_of)
    groups = jnp.stack([(y + shift) % Y for shift in (0, step, -step, 2)])

    tokens = activations.shape[0]
    by_block = activations.reshape(tokens, ROW_BLK, BLOCK)
    kept, received = [], []
    at = 0
    for rows in CHUNKS:
        own = by_block[:, :, at : at + rows].reshape(tokens, ROW_BLK * rows)
        at += rows
        across = move(own, ZL_SWAP)
        near = move(own, X_NEAR)
        back = move(own, X_BACK)
        far = move(near, X_NEAR)
        across_near = move(across, X_NEAR)
        across_back = move(across, X_BACK)
        across_far = move(far, ZL_SWAP)
        pieces = [own, near, back, far, across, across_near, across_back, across_far]
        keep, send = grad_chunk(pieces, rows_of, dest_of, out_grad, rows)
        mine, to_near, to_back, to_far = chip_sum(keep, move(send, C_SWAP), groups)
        parts = [mine, move(to_near, Y_NEAR), move(to_back, Y_BACK), move(to_far, Y_FAR)]
        keep, send = y_sum(parts, zh[None])
        kept.append(keep)
        received.append(move(send, ZH_SWAP))

    roots = root_blocks[0, 0]
    own, grad = apply_roots(kept, received, roots)

    new_stats = statistics_of(grad, statistics[0, 0])
    flag = ((block_at[dp] + stagger_phase[0]) % 8 == 0).astype(jnp.int32)
    new_roots = roots_of(flag[None], new_stats, roots)

    def slot(shift_y, other_z, other_core):
        where_y = (y + shift_y) % Y
        where_z = 1 - zh if other_z else zh
        where_core = 1 - core if other_core else core
        return (where_y * ZH + where_z) * CORE + where_core

    def both_cores(block, shift_y, other_z):
        return [
            (block, block_at[slot(shift_y, other_z, False)]),
            (move(block, C_SWAP), block_at[slot(-shift_y, other_z, True)]),
        ]

    cols = out_grad.shape[1]
    across = move(own, ZH_SWAP)
    near = move(own, Y_NEAR)
    back = move(own, Y_BACK)
    far = move(near, Y_NEAR)
    across_near = move(across, Y_NEAR)
    across_back = move(across, Y_BACK)
    across_far = move(far, ZH_SWAP)
    update = None
    for stage in (
        [(own, 0, False), (across, 0, True), (near, -step, False), (back, step, False)],
        [(far, 2, False), (across_near, -step, True), (across_back, step, True), (across_far, 2, True)],
    ):
        found = [item for entry in stage for item in both_cores(*entry)]
        update = place([b for b, _ in found], [n for _, n in found], update, cols)
    return (update, new_stats[None, None], new_roots[None, None])


def solution(mesh):
    return jax.shard_map(
        body,
        mesh=mesh,
        in_specs=(
            P(("dp", "mp"), None),
            P("dp", "mp"),
            P("mp", "dp", None, None, None),
            P("mp", "dp", None, None, None),
            P("mp", None),
            P("mp"),
        ),
        out_specs=(P(None, "mp"), P("mp", "dp", None, None, None), P("mp", "dp", None, None, None)),
        check_vma=False,
    )
```

```python
import functools

import jax
import jax.numpy as jnp
from jax import lax
from jax.experimental import pallas as pl
from jax.experimental.pallas import tpu as pltpu
from jax.sharding import PartitionSpec as P

FEAT = 4096
BLOCK = 512
ROW_BLK = 8
COL_BLK = 2
BLOCKS = ROW_BLK * COL_BLK
CHUNKS = (256, 256)
Y, ZH, CORE, ZL, X = 4, 2, 2, 2, 4
N_MP = ZL * X
MIB = 1 << 20


def device_of(y, zh, core, zl, x):
    return ((y * ZH + zh) * CORE + core) * N_MP + zl * X + x


def pairs(move):
    out = []
    for y in range(Y):
        for zh in range(ZH):
            for core in range(CORE):
                for zl in range(ZL):
                    for x in range(X):
                        here = (y, zh, core, zl, x)
                        out.append((device_of(*here), device_of(*move(*here))))
    return out


def way(core):
    return 1 if core == 0 else -1


X_NEAR = pairs(lambda y, zh, c, zl, x: (y, zh, c, zl, (x + way(c)) % X))
X_BACK = pairs(lambda y, zh, c, zl, x: (y, zh, c, zl, (x - way(c)) % X))
X_FAR = pairs(lambda y, zh, c, zl, x: (y, zh, c, zl, (x + 2) % X))
Y_NEAR = pairs(lambda y, zh, c, zl, x: ((y + way(c)) % Y, zh, c, zl, x))
Y_BACK = pairs(lambda y, zh, c, zl, x: ((y - way(c)) % Y, zh, c, zl, x))
Y_FAR = pairs(lambda y, zh, c, zl, x: ((y + 2) % Y, zh, c, zl, x))
Y_NEAR_Z = pairs(lambda y, zh, c, zl, x: ((y + way(c)) % Y, 1 - zh, c, zl, x))
Y_BACK_Z = pairs(lambda y, zh, c, zl, x: ((y - way(c)) % Y, 1 - zh, c, zl, x))
Y_FAR_Z = pairs(lambda y, zh, c, zl, x: ((y + 2) % Y, 1 - zh, c, zl, x))
ZL_SWAP = pairs(lambda y, zh, c, zl, x: (y, zh, c, 1 - zl, x))
ZH_SWAP = pairs(lambda y, zh, c, zl, x: (y, 1 - zh, c, zl, x))
C_SWAP = pairs(lambda y, zh, c, zl, x: (y, zh, 1 - c, zl, x))


def move(value, route):
    return lax.ppermute(value, ("dp", "mp"), route)


def cost(flops, moved):
    return pl.CostEstimate(flops=10**12, bytes_accessed=10**12, transcendentals=0)


PARAMS = pltpu.CompilerParams(vmem_limit_bytes=16 * MIB)
ANYWHERE = pl.BlockSpec(memory_space=pl.ANY)
SCALARS = pl.BlockSpec(memory_space=pltpu.SMEM)
WHOLE = pl.BlockSpec(memory_space=pltpu.VMEM)


def mm(a, b, contract):
    return lax.dot_general(a, b, (contract, ((), ())), preferred_element_type=jnp.float32)


def place_here():
    dp, mp = lax.axis_index("dp"), lax.axis_index("mp")
    return dp >> 2, (dp >> 1) & 1, dp & 1, mp >> 2, mp & 3


def hops(core):
    step = 1 - 2 * core
    return 0, -step, step, 2


def block_in(slots, slot):
    number = 0
    for i in range(BLOCKS):
        number = jnp.where(slots[i] == slot, i, number)
    return number


def split(value):
    high = value.astype(jnp.bfloat16)
    return high, (value - high.astype(jnp.float32)).astype(jnp.bfloat16)


def mm3(a, b, contract=((1,), (0,))):
    a_high, a_low = a
    b_high, b_low = b
    return (
        mm(a_high, b_high, contract) + mm(a_high, b_low, contract) + mm(a_low, b_high, contract)
    )


def grad_kernel(rows, span, slots, *refs):
    pieces = refs[:N_MP]
    _, _, core, zl, x = place_here()
    rows_of = [side * X + ((x + hop) & 3) for side in (zl, 1 - zl) for hop in hops(core)]
    og_ref, keep_ref, send_ref, gathered, og, tiles, og_sems, in_sems, sems = refs[N_MP:]
    part = pieces[0].shape[1]
    steps = ROW_BLK // span
    size = span * rows

    def og_copy(col):
        cols = pl.ds(col * BLOCK, BLOCK)
        return pltpu.make_async_copy(og_ref.at[:, cols], og.at[:, cols], og_sems.at[col])

    def piece_copies(step):
        lines = pl.ds(step * size, size)
        return [
            pltpu.make_async_copy(
                pieces[i].at[lines],
                gathered.at[lines, pl.ds(pl.multiple_of(rows_of[i] * part, part), part)],
                in_sems.at[step, i],
            )
            for i in range(N_MP)
        ]

    arrivals = [piece_copies(step) for step in range(steps)]
    for step in range(steps):
        if step < COL_BLK:
            og_copy(step).start()
        for copy in arrivals[step]:
            copy.start()
    for step in range(steps):
        for copy in arrivals[step]:
            copy.wait()
        for col in range(COL_BLK):
            if step == 0:
                og_copy(col).wait()
            grad = mm(
                gathered[step * size : (step + 1) * size],
                og[:, col * BLOCK : (col + 1) * BLOCK],
                ((1,), (0,)),
            ).astype(jnp.bfloat16)
            for row in range(span):
                number = (step * span + row) * COL_BLK + col
                slot = slots[number]
                dest = jnp.where((slot & 1) == core, 0, BLOCKS // 2) + (slot >> 1)
                tiles[number] = grad[row * rows : (row + 1) * rows]

                @pl.when(dest < BLOCKS // 2)
                def _():
                    pltpu.make_async_copy(
                        tiles.at[number], keep_ref.at[dest], sems.at[number]
                    ).start()

                @pl.when(dest >= BLOCKS // 2)
                def _():
                    pltpu.make_async_copy(
                        tiles.at[number], send_ref.at[dest - BLOCKS // 2], sems.at[number]
                    ).start()

    for number in range(BLOCKS):
        pltpu.make_async_copy(tiles.at[number], keep_ref.at[0], sems.at[number]).wait()


def grad_chunk(pieces, slot_of, og, rows):
    tokens, cols = og.shape
    span = 2 if rows > 128 else 4
    steps = ROW_BLK // span
    half = jax.ShapeDtypeStruct((BLOCKS // 2, rows, BLOCK), jnp.bfloat16)
    return pl.pallas_call(
        functools.partial(grad_kernel, rows, span),
        out_shape=(half, half),
        in_specs=[SCALARS] + [ANYWHERE] * (N_MP + 1),
        out_specs=(ANYWHERE, ANYWHERE),
        scratch_shapes=[
            pltpu.VMEM((ROW_BLK * rows, tokens), jnp.bfloat16),
            pltpu.VMEM((tokens, cols), jnp.bfloat16),
            pltpu.VMEM((BLOCKS, rows, BLOCK), jnp.bfloat16),
            pltpu.SemaphoreType.DMA((COL_BLK,)),
            pltpu.SemaphoreType.DMA((steps, N_MP)),
            pltpu.SemaphoreType.DMA((BLOCKS,)),
        ],
        compiler_params=PARAMS,
        cost_estimate=cost(2 * tokens * cols * rows * ROW_BLK, 2 * 5 * MIB),
        name="grad_chunk",
    )(slot_of, *pieces, og)


def chip_kernel(count, by_y, keep_ref, recv_ref, *refs):
    y, zh, core, _, _ = place_here()
    along = [((y - hop) & 3) * ZH for hop in hops(core)]
    if by_y:
        order = [at + j for at in along for j in range(ZH)]
    else:
        order = [at + j for j in (zh, 1 - zh) for at in along]
    outs = refs[:count]
    keep, recv, total, keep_sems, recv_sems, out_sems = refs[count:]
    places = Y * ZH
    each = places // count
    arrivals, copies = [], []
    for i in range(places):
        pair = [
            pltpu.make_async_copy(keep_ref.at[order[i]], keep.at[i], keep_sems.at[i]),
            pltpu.make_async_copy(recv_ref.at[order[i]], recv.at[i], recv_sems.at[i]),
        ]
        for copy in pair:
            copy.start()
        arrivals.append(pair)
    for i in range(places):
        for copy in arrivals[i]:
            copy.wait()
        total[i] = (keep[i].astype(jnp.float32) + recv[i].astype(jnp.float32)).astype(jnp.bfloat16)
        copy = pltpu.make_async_copy(total.at[i], outs[i // each].at[i % each], out_sems.at[i])
        copy.start()
        copies.append(copy)
    for copy in copies:
        copy.wait()


def chip_sum(keep, received, by_y):
    count = Y if by_y else Y * ZH
    rows = keep.shape[1]
    out = jax.ShapeDtypeStruct((Y * ZH // count, rows, BLOCK), jnp.bfloat16)
    held = pltpu.VMEM((Y * ZH, rows, BLOCK), jnp.bfloat16)
    return pl.pallas_call(
        functools.partial(chip_kernel, count, by_y),
        out_shape=(out,) * count,
        in_specs=[ANYWHERE, ANYWHERE],
        out_specs=(ANYWHERE,) * count,
        scratch_shapes=[held] * 3 + [pltpu.SemaphoreType.DMA((Y * ZH,))] * 3,
        compiler_params=PARAMS,
        cost_estimate=cost(MIB, keep.size * 6),
        name="chip_sum",
    )(keep, received)


def y_kernel(*refs):
    _, zh, _, _, _ = place_here()
    parts = refs[:Y]
    keep_ref, send_ref, held, keep, send, in_sems, out_sems = refs[Y:]
    arrivals = []
    for j in range(ZH):
        at = zh if j else 1 - zh
        arrivals.append(
            [pltpu.make_async_copy(parts[i].at[at], held.at[j, i], in_sems.at[j, i]) for i in range(Y)]
        )
        for copy in arrivals[j]:
            copy.start()
    out = [
        pltpu.make_async_copy(send, send_ref, out_sems.at[0]),
        pltpu.make_async_copy(keep, keep_ref, out_sems.at[1]),
    ]
    for j in range(ZH):
        for copy in arrivals[j]:
            copy.wait()
        total = sum(held[j, i].astype(jnp.float32) for i in range(Y))
        if j:
            keep[...] = total
        else:
            send[...] = total.astype(jnp.bfloat16)
        out[j].start()
    for copy in out:
        copy.wait()


def y_sum(parts):
    rows = parts[0].shape[1]
    return pl.pallas_call(
        y_kernel,
        out_shape=(
            jax.ShapeDtypeStruct((rows, BLOCK), jnp.float32),
            jax.ShapeDtypeStruct((rows, BLOCK), jnp.bfloat16),
        ),
        in_specs=[ANYWHERE] * Y,
        out_specs=(ANYWHERE, ANYWHERE),
        scratch_shapes=[
            pltpu.VMEM((ZH, Y, rows, BLOCK), jnp.bfloat16),
            pltpu.VMEM((rows, BLOCK), jnp.float32),
            pltpu.VMEM((rows, BLOCK), jnp.bfloat16),
            pltpu.SemaphoreType.DMA((ZH, Y)),
            pltpu.SemaphoreType.DMA((ZH,)),
        ],
        compiler_params=PARAMS,
        cost_estimate=cost(MIB, rows * BLOCK * 22),
        name="y_sum",
    )(*parts)


def apply_kernel(counts, *refs):
    terms = refs[: sum(counts)]
    roots_ref, update_ref, grad_ref = refs[sum(counts) :]
    at = first = 0
    for rows, count in zip(CHUNKS, counts, strict=True):
        grad_ref[at : at + rows] = sum(
            term[...].astype(jnp.float32) for term in terms[first : first + count]
        )
        at += rows
        first += count
    grad = split(grad_ref[...])
    right = mm3(grad, split(roots_ref[1]))
    update_ref[...] = mm3(split(roots_ref[0]), split(right)).astype(jnp.bfloat16)


def apply_roots(terms, roots):
    counts = [len(group) for group in terms]
    return pl.pallas_call(
        functools.partial(apply_kernel, counts),
        out_shape=(
            jax.ShapeDtypeStruct((BLOCK, BLOCK), jnp.bfloat16),
            jax.ShapeDtypeStruct((BLOCK, BLOCK), jnp.float32),
        ),
        in_specs=[WHOLE] * (sum(counts) + 1),
        out_specs=(WHOLE, WHOLE),
        compiler_params=pltpu.CompilerParams(vmem_limit_bytes=16 * MIB),
        cost_estimate=cost(6 * 2 * BLOCK**3, 5 * MIB),
        name="apply_roots",
    )(*[term for group in terms for term in group], roots)


def stats_kernel(grad_ref, stats_ref, out_ref):
    grad = split(grad_ref[...])
    out_ref[0] = 0.95 * stats_ref[0] + mm3(grad, grad, ((1,), (1,)))
    out_ref[1] = 0.95 * stats_ref[1] + mm3(grad, grad, ((0,), (0,)))


def statistics_of(grad, stats):
    return pl.pallas_call(
        stats_kernel,
        out_shape=jax.ShapeDtypeStruct(stats.shape, jnp.float32),
        in_specs=[WHOLE] * 2,
        out_specs=WHOLE,
        compiler_params=PARAMS,
        cost_estimate=cost(6 * 2 * BLOCK**3, 5 * MIB),
        name="statistics",
    )(grad, stats)


def roots_kernel(slots, phase, stats_ref, roots_ref, out_ref):
    y, zh, core, _, _ = place_here()
    number = block_in(slots, (y * ZH + zh) * CORE + core)
    refreshed = ((number + phase[0]) & 7) == 0

    @pl.when(jnp.logical_not(refreshed))
    def _():
        out_ref[...] = roots_ref[...]

    @pl.when(refreshed)
    def _():
        row = lax.broadcasted_iota(jnp.int32, (BLOCK, BLOCK), 0)
        col = lax.broadcasted_iota(jnp.int32, (BLOCK, BLOCK), 1)
        identity = (row == col).astype(jnp.float32)

        def times(a, b):
            return mm(a.astype(jnp.bfloat16), b.astype(jnp.bfloat16), ((1,), (0,)))

        def powered(coupled):
            rest = times(coupled, coupled) * 0.0625 - 0.625 * coupled
            rest = times(rest, rest) + 3.125 * rest
            return times(rest, coupled) + 2.44140625 * coupled

        for side in range(2):
            matrix = stats_ref[side]
            scaling = 2.5 / jnp.sqrt(jnp.sum(matrix * matrix, keepdims=True))
            first = matrix * scaling
            second = powered(first)
            third = powered(second)
            both = times(first, second) * 0.0625 - 0.3125 * (first + second) + 1.5625 * identity
            found = 1.25 * both - 0.25 * times(both, third)
            out_ref[side] = found * jnp.sqrt(jnp.sqrt(scaling))


def roots_of(slot_of, phase, stats, roots):
    return pl.pallas_call(
        roots_kernel,
        out_shape=jax.ShapeDtypeStruct(stats.shape, jnp.float32),
        in_specs=[SCALARS, SCALARS, WHOLE, WHOLE],
        out_specs=WHOLE,
        compiler_params=PARAMS,
        cost_estimate=cost(16 * 2 * BLOCK**3, 6 * MIB),
        name="roots",
    )(slot_of, phase, stats, roots)


def place_kernel(whence, aliased, slots, *refs):
    y, zh, core, _, _ = place_here()
    count = len(whence)
    blocks = refs[:count]
    out_ref, held, in_sems, out_sems = refs[count + aliased :]
    arrivals = [
        pltpu.make_async_copy(blocks[i], held.at[i], in_sems.at[i]) for i in range(count)
    ]
    for copy in arrivals:
        copy.start()
    copies = []
    for i in range(count):
        hop, other_z, other_core = whence[i]
        there = 1 - core if other_core else core
        at_z = 1 - zh if other_z else zh
        number = block_in(slots, (((y + hops(there)[hop]) & 3) * ZH + at_z) * CORE + there)
        row = pl.multiple_of(number // COL_BLK * BLOCK, BLOCK)
        col = pl.multiple_of(number % COL_BLK * BLOCK, BLOCK)
        arrivals[i].wait()
        copy = pltpu.make_async_copy(
            held.at[i], out_ref.at[pl.ds(row, BLOCK), pl.ds(col, BLOCK)], out_sems.at[i]
        )
        copy.start()
        copies.append(copy)
    for copy in copies:
        copy.wait()


def place(found, slot_of, into, cols):
    blocks, whence = [entry[0] for entry in found], [entry[1:] for entry in found]
    count = len(found)
    aliased = into is not None
    return pl.pallas_call(
        functools.partial(place_kernel, whence, int(aliased)),
        out_shape=jax.ShapeDtypeStruct((FEAT, cols), jnp.bfloat16),
        in_specs=[SCALARS] + [ANYWHERE] * (count + aliased),
        out_specs=ANYWHERE,
        scratch_shapes=[
            pltpu.VMEM((count, BLOCK, BLOCK), jnp.bfloat16),
            pltpu.SemaphoreType.DMA((count,)),
            pltpu.SemaphoreType.DMA((count,)),
        ],
        input_output_aliases={count + 1: 0} if aliased else {},
        compiler_params=PARAMS,
        cost_estimate=cost(0, count * MIB),
        name="place",
    )(slot_of, *blocks, *([into] if aliased else []))


def after(value, *others):
    return lax.optimization_barrier((value, *others))[0]


def body(activations, out_grad, statistics, root_blocks, owner_slots, stagger_phase):
    slot_of = owner_slots[0]
    roots = root_blocks[0, 0]
    tokens = activations.shape[0]
    cols = out_grad.shape[1]
    by_block = activations.reshape(tokens, ROW_BLK, BLOCK)
    owns = []
    at = 0
    for rows in CHUNKS:
        owns.append(by_block[:, :, at : at + rows].transpose(1, 2, 0).reshape(ROW_BLK * rows, tokens))
        at += rows

    far_a, across_a = move(owns[0], X_FAR), move(owns[0], ZL_SWAP)
    near_a, back_a = move(owns[0], X_NEAR), move(owns[0], X_BACK)
    across_b = move(after(owns[1], across_a), ZL_SWAP)
    rest_a = [move(across_a, X_NEAR), move(across_a, X_BACK), move(far_a, ZL_SWAP)]
    rest_a[2] = after(rest_a[2], across_b)
    own_b = after(owns[1], far_a)
    far_b, near_b, back_b = move(own_b, X_FAR), move(own_b, X_NEAR), move(own_b, X_BACK)

    pieces = [owns[0], near_a, back_a, far_a, across_a, *rest_a]
    keep_a, send_a = grad_chunk(pieces, slot_of, out_grad, CHUNKS[0])
    swapped_a = move(after(send_a, near_b, back_b), C_SWAP)
    across_b = after(across_b, keep_a)
    rest_b = [move(across_b, X_NEAR), move(across_b, X_BACK), move(far_b, ZL_SWAP)]
    mine, *to = chip_sum(keep_a, swapped_a, True)
    parts = [mine, move(to[0], Y_NEAR), move(to[1], Y_BACK), move(to[2], Y_FAR)]

    pieces = [owns[1], near_b, back_b, far_b, across_b, *rest_b]
    keep_b, send_b = grad_chunk(pieces, slot_of, out_grad, CHUNKS[1])
    swapped_b = move(after(send_b, *parts[1:]), C_SWAP)
    keep_a, send_a = y_sum(parts)
    mine, *to = chip_sum(keep_b, after(swapped_b, send_a), False)
    to = [part[0] for part in to]
    near, back, far = move(to[0], Y_NEAR), move(to[1], Y_BACK), move(to[2], Y_FAR)
    terms_b = [mine[0], near, back, far, move(to[3], ZH_SWAP), move(to[6], Y_FAR_Z)]
    terms_b += [move(after(to[4], near), Y_NEAR_Z), move(after(to[5], back), Y_BACK_Z)]
    terms_a = [keep_a, move(send_a, ZH_SWAP)]

    own, grad = apply_roots([terms_a, terms_b], roots)

    across, near, back = move(own, ZH_SWAP), move(own, Y_NEAR), move(own, Y_BACK)
    own_other = move(own, C_SWAP)
    new_stats = statistics_of(grad, statistics[0, 0])
    near = after(near, new_stats, own_other)
    far = move(near, Y_NEAR)
    across, far_ = after(across, far), after(far, back)
    across_near, across_back = move(across, Y_NEAR), move(across, Y_BACK)
    across_far = move(far_, ZH_SWAP)
    new_roots = roots_of(slot_of, stagger_phase, after(new_stats, far), roots)
    found = [(own, 0, False, False), (own_other, 0, False, True)]
    found += [(near, 1, False, False), (move(near, C_SWAP), 1, False, True)]
    found += [(back, 2, False, False), (move(back, C_SWAP), 2, False, True)]
    found += [(across, 0, True, False), (far, 3, False, False)]
    update = place(found, slot_of, None, cols)

    found = []
    for block, hop in ((across_near, 1), (across_back, 2), (across_far, 3)):
        block = after(block, update, new_roots)
        found += [(block, hop, True, False), (move(block, C_SWAP), hop, True, True)]
    found.append((move(after(across, update, new_roots), C_SWAP), 0, True, True))
    found.append((move(after(far, update, new_roots), C_SWAP), 3, False, True))
    update = place(found, slot_of, update, cols)
    return (update, new_stats[None, None], new_roots[None, None])


def solution(mesh):
    return jax.shard_map(
        body,
        mesh=mesh,
        in_specs=(
            P(("dp", "mp"), None),
            P("dp", "mp"),
            P("mp", "dp", None, None, None),
            P("mp", "dp", None, None, None),
            P("mp", None),
            P("mp"),
        ),
        out_specs=(P(None, "mp"), P("mp", "dp", None, None, None), P("mp", "dp", None, None, None)),
        check_vma=False,
    )
```

```python
import functools

import jax
import jax.numpy as jnp
from jax import lax
from jax.experimental import pallas as pl
from jax.experimental.pallas import tpu as pltpu
from jax.sharding import PartitionSpec as P

FEAT = 4096
BLOCK = 512
ROW_BLK = 8
COL_BLK = 2
BLOCKS = ROW_BLK * COL_BLK
CHUNKS = (256, 256)
Y, ZH, CORE, ZL, X = 4, 2, 2, 2, 4
N_MP = ZL * X
MIB = 1 << 20


def device_of(y, zh, core, zl, x):
    return ((y * ZH + zh) * CORE + core) * N_MP + zl * X + x


def pairs(move):
    out = []
    for y in range(Y):
        for zh in range(ZH):
            for core in range(CORE):
                for zl in range(ZL):
                    for x in range(X):
                        here = (y, zh, core, zl, x)
                        out.append((device_of(*here), device_of(*move(*here))))
    return out


def way(core):
    return 1 if core == 0 else -1


X_NEAR = pairs(lambda y, zh, c, zl, x: (y, zh, c, zl, (x + way(c)) % X))
X_BACK = pairs(lambda y, zh, c, zl, x: (y, zh, c, zl, (x - way(c)) % X))
X_FAR = pairs(lambda y, zh, c, zl, x: (y, zh, c, zl, (x + 2) % X))
Y_NEAR = pairs(lambda y, zh, c, zl, x: ((y + way(c)) % Y, zh, c, zl, x))
Y_BACK = pairs(lambda y, zh, c, zl, x: ((y - way(c)) % Y, zh, c, zl, x))
Y_FAR = pairs(lambda y, zh, c, zl, x: ((y + 2) % Y, zh, c, zl, x))
Y_NEAR_Z = pairs(lambda y, zh, c, zl, x: ((y + way(c)) % Y, 1 - zh, c, zl, x))
Y_BACK_Z = pairs(lambda y, zh, c, zl, x: ((y - way(c)) % Y, 1 - zh, c, zl, x))
Y_FAR_Z = pairs(lambda y, zh, c, zl, x: ((y + 2) % Y, 1 - zh, c, zl, x))
ZL_SWAP = pairs(lambda y, zh, c, zl, x: (y, zh, c, 1 - zl, x))
ZH_SWAP = pairs(lambda y, zh, c, zl, x: (y, 1 - zh, c, zl, x))
C_SWAP = pairs(lambda y, zh, c, zl, x: (y, zh, 1 - c, zl, x))


def move(value, route):
    return lax.ppermute(value, ("dp", "mp"), route)


def cost(micros):
    return pl.CostEstimate(flops=int(micros * 1.15e9), bytes_accessed=1024, transcendentals=0)


PARAMS = pltpu.CompilerParams(vmem_limit_bytes=16 * MIB)
ANYWHERE = pl.BlockSpec(memory_space=pl.ANY)
SCALARS = pl.BlockSpec(memory_space=pltpu.SMEM)
WHOLE = pl.BlockSpec(memory_space=pltpu.VMEM)


def mm(a, b, contract):
    return lax.dot_general(a, b, (contract, ((), ())), preferred_element_type=jnp.float32)


def place_here():
    dp, mp = lax.axis_index("dp"), lax.axis_index("mp")
    return dp >> 2, (dp >> 1) & 1, dp & 1, mp >> 2, mp & 3


def hops(core):
    step = 1 - 2 * core
    return 0, -step, step, 2


def block_in(slots, slot):
    number = 0
    for i in range(BLOCKS):
        number = jnp.where(slots[i] == slot, i, number)
    return number


def split(value):
    high = value.astype(jnp.bfloat16)
    return high, (value - high.astype(jnp.float32)).astype(jnp.bfloat16)


def mm3(a, b, contract=((1,), (0,))):
    a_high, a_low = a
    b_high, b_low = b
    return (
        mm(a_high, b_high, contract) + mm(a_high, b_low, contract) + mm(a_low, b_high, contract)
    )


def grad_kernel(rows, span, slots, *refs):
    pieces = refs[:N_MP]
    _, _, core, zl, x = place_here()
    rows_of = [side * X + ((x + hop) & 3) for side in (zl, 1 - zl) for hop in hops(core)]
    og_ref, keep_ref, send_ref, gathered, og, tiles, og_sems, in_sems, sems = refs[N_MP:]
    part = pieces[0].shape[1]
    steps = ROW_BLK // span
    size = span * rows

    def og_copy(col):
        cols = pl.ds(col * BLOCK, BLOCK)
        return pltpu.make_async_copy(og_ref.at[:, cols], og.at[:, cols], og_sems.at[col])

    def piece_copies(step):
        lines = pl.ds(step * size, size)
        return [
            pltpu.make_async_copy(
                pieces[i].at[lines],
                gathered.at[lines, pl.ds(pl.multiple_of(rows_of[i] * part, part), part)],
                in_sems.at[step, i],
            )
            for i in range(N_MP)
        ]

    arrivals = [piece_copies(step) for step in range(steps)]
    for step in range(steps):
        if step < COL_BLK:
            og_copy(step).start()
        for copy in arrivals[step]:
            copy.start()
    for step in range(steps):
        for copy in arrivals[step]:
            copy.wait()
        for col in range(COL_BLK):
            if step == 0:
                og_copy(col).wait()
            grad = mm(
                gathered[step * size : (step + 1) * size],
                og[:, col * BLOCK : (col + 1) * BLOCK],
                ((1,), (0,)),
            ).astype(jnp.bfloat16)
            for row in range(span):
                number = (step * span + row) * COL_BLK + col
                slot = slots[number]
                dest = jnp.where((slot & 1) == core, 0, BLOCKS // 2) + (slot >> 1)
                tiles[number] = grad[row * rows : (row + 1) * rows]

                @pl.when(dest < BLOCKS // 2)
                def _():
                    pltpu.make_async_copy(
                        tiles.at[number], keep_ref.at[dest], sems.at[number]
                    ).start()

                @pl.when(dest >= BLOCKS // 2)
                def _():
                    pltpu.make_async_copy(
                        tiles.at[number], send_ref.at[dest - BLOCKS // 2], sems.at[number]
                    ).start()

    for number in range(BLOCKS):
        pltpu.make_async_copy(tiles.at[number], keep_ref.at[0], sems.at[number]).wait()


def grad_chunk(pieces, slot_of, og, rows):
    tokens, cols = og.shape
    span = 2 if rows > 128 else 4
    steps = ROW_BLK // span
    half = jax.ShapeDtypeStruct((BLOCKS // 2, rows, BLOCK), jnp.bfloat16)
    return pl.pallas_call(
        functools.partial(grad_kernel, rows, span),
        out_shape=(half, half),
        in_specs=[SCALARS] + [ANYWHERE] * (N_MP + 1),
        out_specs=(ANYWHERE, ANYWHERE),
        scratch_shapes=[
            pltpu.VMEM((ROW_BLK * rows, tokens), jnp.bfloat16),
            pltpu.VMEM((tokens, cols), jnp.bfloat16),
            pltpu.VMEM((BLOCKS, rows, BLOCK), jnp.bfloat16),
            pltpu.SemaphoreType.DMA((COL_BLK,)),
            pltpu.SemaphoreType.DMA((steps, N_MP)),
            pltpu.SemaphoreType.DMA((BLOCKS,)),
        ],
        compiler_params=PARAMS,
        cost_estimate=cost(rows / 30),
        name="grad_chunk",
    )(slot_of, *pieces, og)


def chip_kernel(count, by_y, keep_ref, recv_ref, *refs):
    y, zh, core, _, _ = place_here()
    along = [((y - hop) & 3) * ZH for hop in hops(core)]
    if by_y:
        order = [at + j for at in along for j in range(ZH)]
    else:
        order = [at + j for j in (zh, 1 - zh) for at in along]
    outs = refs[:count]
    keep, recv, total, keep_sems, recv_sems, out_sems = refs[count:]
    places = Y * ZH
    each = places // count
    arrivals, copies = [], []
    for i in range(places):
        pair = [
            pltpu.make_async_copy(keep_ref.at[order[i]], keep.at[i], keep_sems.at[i]),
            pltpu.make_async_copy(recv_ref.at[order[i]], recv.at[i], recv_sems.at[i]),
        ]
        for copy in pair:
            copy.start()
        arrivals.append(pair)
    for i in range(places):
        for copy in arrivals[i]:
            copy.wait()
        total[i] = (keep[i].astype(jnp.float32) + recv[i].astype(jnp.float32)).astype(jnp.bfloat16)
        copy = pltpu.make_async_copy(total.at[i], outs[i // each].at[i % each], out_sems.at[i])
        copy.start()
        copies.append(copy)
    for copy in copies:
        copy.wait()


def chip_sum(keep, received, by_y):
    count = Y if by_y else Y * ZH
    rows = keep.shape[1]
    out = jax.ShapeDtypeStruct((Y * ZH // count, rows, BLOCK), jnp.bfloat16)
    held = pltpu.VMEM((Y * ZH, rows, BLOCK), jnp.bfloat16)
    return pl.pallas_call(
        functools.partial(chip_kernel, count, by_y),
        out_shape=(out,) * count,
        in_specs=[ANYWHERE, ANYWHERE],
        out_specs=(ANYWHERE,) * count,
        scratch_shapes=[held] * 3 + [pltpu.SemaphoreType.DMA((Y * ZH,))] * 3,
        compiler_params=PARAMS,
        cost_estimate=cost(1.9),
        name="chip_sum",
    )(keep, received)


def y_kernel(*refs):
    _, zh, _, _, _ = place_here()
    parts = refs[:Y]
    keep_ref, send_ref, held, keep, send, in_sems, out_sems = refs[Y:]
    arrivals = []
    for j in range(ZH):
        at = zh if j else 1 - zh
        arrivals.append(
            [pltpu.make_async_copy(parts[i].at[at], held.at[j, i], in_sems.at[j, i]) for i in range(Y)]
        )
        for copy in arrivals[j]:
            copy.start()
    out = [
        pltpu.make_async_copy(send, send_ref, out_sems.at[0]),
        pltpu.make_async_copy(keep, keep_ref, out_sems.at[1]),
    ]
    for j in range(ZH):
        for copy in arrivals[j]:
            copy.wait()
        total = sum(held[j, i].astype(jnp.float32) for i in range(Y))
        if j:
            keep[...] = total
        else:
            send[...] = total.astype(jnp.bfloat16)
        out[j].start()
    for copy in out:
        copy.wait()


def y_sum(parts):
    rows = parts[0].shape[1]
    return pl.pallas_call(
        y_kernel,
        out_shape=(
            jax.ShapeDtypeStruct((rows, BLOCK), jnp.float32),
            jax.ShapeDtypeStruct((rows, BLOCK), jnp.bfloat16),
        ),
        in_specs=[ANYWHERE] * Y,
        out_specs=(ANYWHERE, ANYWHERE),
        scratch_shapes=[
            pltpu.VMEM((ZH, Y, rows, BLOCK), jnp.bfloat16),
            pltpu.VMEM((rows, BLOCK), jnp.float32),
            pltpu.VMEM((rows, BLOCK), jnp.bfloat16),
            pltpu.SemaphoreType.DMA((ZH, Y)),
            pltpu.SemaphoreType.DMA((ZH,)),
        ],
        compiler_params=PARAMS,
        cost_estimate=cost(1.8),
        name="y_sum",
    )(*parts)


def apply_kernel(counts, *refs):
    terms = refs[: sum(counts)]
    roots_ref, update_ref, grad_ref = refs[sum(counts) :]
    at = first = 0
    for rows, count in zip(CHUNKS, counts, strict=True):
        grad_ref[at : at + rows] = sum(
            term[...].astype(jnp.float32) for term in terms[first : first + count]
        )
        at += rows
        first += count
    grad = split(grad_ref[...])
    right = mm3(grad, split(roots_ref[1]))
    update_ref[...] = mm3(split(roots_ref[0]), split(right)).astype(jnp.bfloat16)


def apply_roots(terms, roots):
    counts = [len(group) for group in terms]
    return pl.pallas_call(
        functools.partial(apply_kernel, counts),
        out_shape=(
            jax.ShapeDtypeStruct((BLOCK, BLOCK), jnp.bfloat16),
            jax.ShapeDtypeStruct((BLOCK, BLOCK), jnp.float32),
        ),
        in_specs=[WHOLE] * (sum(counts) + 1),
        out_specs=(WHOLE, WHOLE),
        compiler_params=pltpu.CompilerParams(vmem_limit_bytes=16 * MIB),
        cost_estimate=cost(2.8),
        name="apply_roots",
    )(*[term for group in terms for term in group], roots)


def stats_kernel(grad_ref, stats_ref, out_ref):
    grad = split(grad_ref[...])
    out_ref[0] = 0.95 * stats_ref[0] + mm3(grad, grad, ((1,), (1,)))
    out_ref[1] = 0.95 * stats_ref[1] + mm3(grad, grad, ((0,), (0,)))


def statistics_of(grad, stats):
    return pl.pallas_call(
        stats_kernel,
        out_shape=jax.ShapeDtypeStruct(stats.shape, jnp.float32),
        in_specs=[WHOLE] * 2,
        out_specs=WHOLE,
        compiler_params=PARAMS,
        cost_estimate=cost(3.2),
        name="statistics",
    )(grad, stats)


def roots_kernel(slots, phase, stats_ref, roots_ref, out_ref):
    y, zh, core, _, _ = place_here()
    number = block_in(slots, (y * ZH + zh) * CORE + core)
    refreshed = ((number + phase[0]) & 7) == 0

    @pl.when(jnp.logical_not(refreshed))
    def _():
        out_ref[...] = roots_ref[...]

    @pl.when(refreshed)
    def _():
        row = lax.broadcasted_iota(jnp.int32, (BLOCK, BLOCK), 0)
        col = lax.broadcasted_iota(jnp.int32, (BLOCK, BLOCK), 1)
        identity = (row == col).astype(jnp.float32)

        def times(a, b):
            return mm(a.astype(jnp.bfloat16), b.astype(jnp.bfloat16), ((1,), (0,)))

        def powered(coupled):
            rest = times(coupled, coupled) * 0.0625 - 0.625 * coupled
            rest = times(rest, rest) + 3.125 * rest
            return times(rest, coupled) + 2.44140625 * coupled

        for side in range(2):
            matrix = stats_ref[side]
            scaling = 2.5 / jnp.sqrt(jnp.sum(matrix * matrix, keepdims=True))
            first = matrix * scaling
            second = powered(first)
            third = powered(second)
            both = times(first, second) * 0.0625 - 0.3125 * (first + second) + 1.5625 * identity
            found = 1.25 * both - 0.25 * times(both, third)
            out_ref[side] = found * jnp.sqrt(jnp.sqrt(scaling))


def roots_of(slot_of, phase, stats, roots):
    return pl.pallas_call(
        roots_kernel,
        out_shape=jax.ShapeDtypeStruct(stats.shape, jnp.float32),
        in_specs=[SCALARS, SCALARS, WHOLE, WHOLE],
        out_specs=WHOLE,
        compiler_params=PARAMS,
        cost_estimate=cost(4.0),
        name="roots",
    )(slot_of, phase, stats, roots)


def place_kernel(whence, aliased, slots, *refs):
    y, zh, core, _, _ = place_here()
    count = len(whence)
    blocks = refs[:count]
    out_ref, held, in_sems, out_sems = refs[count + aliased :]
    arrivals = [
        pltpu.make_async_copy(blocks[i], held.at[i], in_sems.at[i]) for i in range(count)
    ]
    for copy in arrivals:
        copy.start()
    copies = []
    for i in range(count):
        hop, other_z, other_core = whence[i]
        there = 1 - core if other_core else core
        at_z = 1 - zh if other_z else zh
        number = block_in(slots, (((y + hops(there)[hop]) & 3) * ZH + at_z) * CORE + there)
        row = pl.multiple_of(number // COL_BLK * BLOCK, BLOCK)
        col = pl.multiple_of(number % COL_BLK * BLOCK, BLOCK)
        arrivals[i].wait()
        copy = pltpu.make_async_copy(
            held.at[i], out_ref.at[pl.ds(row, BLOCK), pl.ds(col, BLOCK)], out_sems.at[i]
        )
        copy.start()
        copies.append(copy)
    for copy in copies:
        copy.wait()


def place(found, slot_of, into, cols):
    blocks, whence = [entry[0] for entry in found], [entry[1:] for entry in found]
    count = len(found)
    aliased = into is not None
    return pl.pallas_call(
        functools.partial(place_kernel, whence, int(aliased)),
        out_shape=jax.ShapeDtypeStruct((FEAT, cols), jnp.bfloat16),
        in_specs=[SCALARS] + [ANYWHERE] * (count + aliased),
        out_specs=ANYWHERE,
        scratch_shapes=[
            pltpu.VMEM((count, BLOCK, BLOCK), jnp.bfloat16),
            pltpu.SemaphoreType.DMA((count,)),
            pltpu.SemaphoreType.DMA((count,)),
        ],
        input_output_aliases={count + 1: 0} if aliased else {},
        compiler_params=PARAMS,
        cost_estimate=cost(3.7),
        name="place",
    )(slot_of, *blocks, *([into] if aliased else []))


def after(value, *others):
    return lax.optimization_barrier((value, *others))[0]


def body(activations, out_grad, statistics, root_blocks, owner_slots, stagger_phase):
    slot_of = owner_slots[0]
    roots = root_blocks[0, 0]
    tokens = activations.shape[0]
    cols = out_grad.shape[1]
    by_block = activations.reshape(tokens, ROW_BLK, BLOCK)
    owns = []
    at = 0
    for rows in CHUNKS:
        owns.append(by_block[:, :, at : at + rows].transpose(1, 2, 0).reshape(ROW_BLK * rows, tokens))
        at += rows

    far_a, across_a = move(owns[0], X_FAR), move(owns[0], ZL_SWAP)
    near_a, back_a = move(owns[0], X_NEAR), move(owns[0], X_BACK)
    across_b = move(after(owns[1], across_a), ZL_SWAP)
    rest_a = [move(across_a, X_NEAR), move(across_a, X_BACK), move(far_a, ZL_SWAP)]
    own_b = after(owns[1], far_a)
    near_b, back_b = move(own_b, X_NEAR), move(own_b, X_BACK)

    pieces = [owns[0], near_a, back_a, far_a, across_a, *rest_a]
    keep_a, send_a = grad_chunk(pieces, slot_of, out_grad, CHUNKS[0])
    swapped_a = move(after(send_a, near_b, back_b, across_b), C_SWAP)
    across_b = after(across_b, keep_a)
    far_b = move(after(near_b, keep_a), X_NEAR)
    mine, *to = chip_sum(keep_a, swapped_a, True)
    rest_b = [move(across_b, X_NEAR), move(across_b, X_BACK), move(after(far_b, mine), ZL_SWAP)]
    parts = [mine, move(to[0], Y_NEAR), move(to[1], Y_BACK), move(to[2], Y_FAR)]

    rest_b[0] = after(rest_b[0], parts[1], parts[2])
    pieces = [owns[1], near_b, back_b, far_b, across_b, *rest_b]
    keep_b, send_b = grad_chunk(pieces, slot_of, out_grad, CHUNKS[1])
    swapped_b = move(after(send_b, *parts[1:]), C_SWAP)
    keep_a, send_a = y_sum(parts)
    mine, *to = chip_sum(keep_b, after(swapped_b, send_a), False)
    to = [part[0] for part in to]
    near, back, far = move(to[0], Y_NEAR), move(to[1], Y_BACK), move(to[2], Y_FAR)
    terms_b = [mine[0], near, back, far, move(to[3], ZH_SWAP), move(to[6], Y_FAR_Z)]
    terms_b += [move(to[4], Y_NEAR_Z), move(to[5], Y_BACK_Z)]
    terms_a = [keep_a, move(send_a, ZH_SWAP)]

    own, grad = apply_roots([terms_a, terms_b], roots)

    across, near, back = move(own, ZH_SWAP), move(own, Y_NEAR), move(own, Y_BACK)
    own_other = move(own, C_SWAP)
    new_stats = statistics_of(grad, statistics[0, 0])
    near = after(near, new_stats, own_other)
    far = move(near, Y_NEAR)
    across, far_ = after(across, far), after(far, back)
    across_near, across_back = move(across, Y_NEAR), move(across, Y_BACK)
    across_far = move(far_, ZH_SWAP)
    new_roots = roots_of(slot_of, stagger_phase, after(new_stats, far), roots)
    found = [(own, 0, False, False), (own_other, 0, False, True)]
    found += [(near, 1, False, False), (move(near, C_SWAP), 1, False, True)]
    found += [(back, 2, False, False), (move(back, C_SWAP), 2, False, True)]
    found += [(across, 0, True, False), (far, 3, False, False)]
    update = place(found, slot_of, None, cols)

    found = []
    for block, hop in ((across_near, 1), (across_back, 2), (across_far, 3)):
        block = after(block, update, new_roots)
        found += [(block, hop, True, False), (move(block, C_SWAP), hop, True, True)]
    found.append((move(after(across, update, new_roots), C_SWAP), 0, True, True))
    found.append((move(after(far, update, new_roots), C_SWAP), 3, False, True))
    update = place(found, slot_of, update, cols)
    return (update, new_stats[None, None], new_roots[None, None])


def solution(mesh):
    return jax.shard_map(
        body,
        mesh=mesh,
        in_specs=(
            P(("dp", "mp"), None),
            P("dp", "mp"),
            P("mp", "dp", None, None, None),
            P("mp", "dp", None, None, None),
            P("mp", None),
            P("mp"),
        ),
        out_specs=(P(None, "mp"), P("mp", "dp", None, None, None), P("mp", "dp", None, None, None)),
        check_vma=False,
    )
```

```python
import functools

import jax
import jax.numpy as jnp
from jax import lax
from jax.experimental import pallas as pl
from jax.experimental.pallas import tpu as pltpu
from jax.sharding import PartitionSpec as P

FEAT = 4096
BLOCK = 512
ROW_BLK = 8
COL_BLK = 2
BLOCKS = ROW_BLK * COL_BLK
CHUNKS = (256, 256)
Y, ZH, CORE, ZL, X = 4, 2, 2, 2, 4
N_MP = ZL * X
MIB = 1 << 20


def device_of(y, zh, core, zl, x):
    return ((y * ZH + zh) * CORE + core) * N_MP + zl * X + x


def pairs(move):
    out = []
    for y in range(Y):
        for zh in range(ZH):
            for core in range(CORE):
                for zl in range(ZL):
                    for x in range(X):
                        here = (y, zh, core, zl, x)
                        out.append((device_of(*here), device_of(*move(*here))))
    return out


def way(core):
    return 1 if core == 0 else -1


X_NEAR = pairs(lambda y, zh, c, zl, x: (y, zh, c, zl, (x + way(c)) % X))
X_BACK = pairs(lambda y, zh, c, zl, x: (y, zh, c, zl, (x - way(c)) % X))
X_FAR = pairs(lambda y, zh, c, zl, x: (y, zh, c, zl, (x + 2) % X))
Y_NEAR = pairs(lambda y, zh, c, zl, x: ((y + way(c)) % Y, zh, c, zl, x))
Y_BACK = pairs(lambda y, zh, c, zl, x: ((y - way(c)) % Y, zh, c, zl, x))
Y_FAR = pairs(lambda y, zh, c, zl, x: ((y + 2) % Y, zh, c, zl, x))
Y_NEAR_Z = pairs(lambda y, zh, c, zl, x: ((y + way(c)) % Y, 1 - zh, c, zl, x))
Y_BACK_Z = pairs(lambda y, zh, c, zl, x: ((y - way(c)) % Y, 1 - zh, c, zl, x))
Y_FAR_Z = pairs(lambda y, zh, c, zl, x: ((y + 2) % Y, 1 - zh, c, zl, x))
ZL_SWAP = pairs(lambda y, zh, c, zl, x: (y, zh, c, 1 - zl, x))
ZH_SWAP = pairs(lambda y, zh, c, zl, x: (y, 1 - zh, c, zl, x))
C_SWAP = pairs(lambda y, zh, c, zl, x: (y, zh, 1 - c, zl, x))


def move(value, route):
    return lax.ppermute(value, ("dp", "mp"), route)


def cost(micros):
    return pl.CostEstimate(flops=int(micros * 1.15e9), bytes_accessed=1024, transcendentals=0)


PARAMS = pltpu.CompilerParams(vmem_limit_bytes=16 * MIB)
ANYWHERE = pl.BlockSpec(memory_space=pl.ANY)
SCALARS = pl.BlockSpec(memory_space=pltpu.SMEM)
WHOLE = pl.BlockSpec(memory_space=pltpu.VMEM)


def mm(a, b, contract):
    return lax.dot_general(a, b, (contract, ((), ())), preferred_element_type=jnp.float32)


def place_here():
    dp, mp = lax.axis_index("dp"), lax.axis_index("mp")
    return dp >> 2, (dp >> 1) & 1, dp & 1, mp >> 2, mp & 3


def hops(core):
    step = 1 - 2 * core
    return 0, -step, step, 2


def block_in(slots, slot):
    number = 0
    for i in range(BLOCKS):
        number = jnp.where(slots[i] == slot, i, number)
    return number


def split(value):
    high = value.astype(jnp.bfloat16)
    return high, (value - high.astype(jnp.float32)).astype(jnp.bfloat16)


def mm3(a, b, contract=((1,), (0,))):
    a_high, a_low = a
    b_high, b_low = b
    return (
        mm(a_high, b_high, contract) + mm(a_high, b_low, contract) + mm(a_low, b_high, contract)
    )


def grad_kernel(rows, span, slots, *refs):
    pieces = refs[:N_MP]
    _, _, core, zl, x = place_here()
    rows_of = [side * X + ((x + hop) & 3) for side in (zl, 1 - zl) for hop in hops(core)]
    og_ref, keep_ref, send_ref, gathered, og, tiles, og_sems, in_sems, sems = refs[N_MP:]
    part = pieces[0].shape[1]
    steps = ROW_BLK // span
    size = span * rows

    def og_copy(col):
        cols = pl.ds(col * BLOCK, BLOCK)
        return pltpu.make_async_copy(og_ref.at[:, cols], og.at[:, cols], og_sems.at[col])

    def piece_copies(step):
        lines = pl.ds(step * size, size)
        return [
            pltpu.make_async_copy(
                pieces[i].at[lines],
                gathered.at[lines, pl.ds(pl.multiple_of(rows_of[i] * part, part), part)],
                in_sems.at[step, i],
            )
            for i in range(N_MP)
        ]

    arrivals = [piece_copies(step) for step in range(steps)]
    for step in range(steps):
        if step < COL_BLK:
            og_copy(step).start()
        for copy in arrivals[step]:
            copy.start()
    for step in range(steps):
        for copy in arrivals[step]:
            copy.wait()
        for col in range(COL_BLK):
            if step == 0:
                og_copy(col).wait()
            grad = mm(
                gathered[step * size : (step + 1) * size],
                og[:, col * BLOCK : (col + 1) * BLOCK],
                ((1,), (0,)),
            ).astype(jnp.bfloat16)
            for row in range(span):
                number = (step * span + row) * COL_BLK + col
                slot = slots[number]
                dest = jnp.where((slot & 1) == core, 0, BLOCKS // 2) + (slot >> 1)
                tiles[number] = grad[row * rows : (row + 1) * rows]

                @pl.when(dest < BLOCKS // 2)
                def _():
                    pltpu.make_async_copy(
                        tiles.at[number], keep_ref.at[dest], sems.at[number]
                    ).start()

                @pl.when(dest >= BLOCKS // 2)
                def _():
                    pltpu.make_async_copy(
                        tiles.at[number], send_ref.at[dest - BLOCKS // 2], sems.at[number]
                    ).start()

    for number in range(BLOCKS):
        pltpu.make_async_copy(tiles.at[number], keep_ref.at[0], sems.at[number]).wait()


def grad_chunk(pieces, slot_of, og, rows):
    tokens, cols = og.shape
    span = 2 if rows > 128 else 4
    steps = ROW_BLK // span
    half = jax.ShapeDtypeStruct((BLOCKS // 2, rows, BLOCK), jnp.bfloat16)
    return pl.pallas_call(
        functools.partial(grad_kernel, rows, span),
        out_shape=(half, half),
        in_specs=[SCALARS] + [ANYWHERE] * (N_MP + 1),
        out_specs=(ANYWHERE, ANYWHERE),
        scratch_shapes=[
            pltpu.VMEM((ROW_BLK * rows, tokens), jnp.bfloat16),
            pltpu.VMEM((tokens, cols), jnp.bfloat16),
            pltpu.VMEM((BLOCKS, rows, BLOCK), jnp.bfloat16),
            pltpu.SemaphoreType.DMA((COL_BLK,)),
            pltpu.SemaphoreType.DMA((steps, N_MP)),
            pltpu.SemaphoreType.DMA((BLOCKS,)),
        ],
        compiler_params=PARAMS,
        cost_estimate=cost(rows / 30),
        name="grad_chunk",
    )(slot_of, *pieces, og)


def chip_kernel(count, by_y, keep_ref, recv_ref, *refs):
    y, zh, core, _, _ = place_here()
    along = [((y - hop) & 3) * ZH for hop in hops(core)]
    if by_y:
        order = [at + j for at in along for j in range(ZH)]
    else:
        order = [at + j for j in (zh, 1 - zh) for at in along]
    outs = refs[:count]
    keep, recv, total, keep_sems, recv_sems, out_sems = refs[count:]
    places = Y * ZH
    each = places // count
    arrivals, copies = [], []
    for i in range(places):
        pair = [
            pltpu.make_async_copy(keep_ref.at[order[i]], keep.at[i], keep_sems.at[i]),
            pltpu.make_async_copy(recv_ref.at[order[i]], recv.at[i], recv_sems.at[i]),
        ]
        for copy in pair:
            copy.start()
        arrivals.append(pair)
    for i in range(places):
        for copy in arrivals[i]:
            copy.wait()
        total[i] = (keep[i].astype(jnp.float32) + recv[i].astype(jnp.float32)).astype(jnp.bfloat16)
        copy = pltpu.make_async_copy(total.at[i], outs[i // each].at[i % each], out_sems.at[i])
        copy.start()
        copies.append(copy)
    for copy in copies:
        copy.wait()


def chip_sum(keep, received, by_y):
    count = Y if by_y else Y * ZH
    rows = keep.shape[1]
    out = jax.ShapeDtypeStruct((Y * ZH // count, rows, BLOCK), jnp.bfloat16)
    held = pltpu.VMEM((Y * ZH, rows, BLOCK), jnp.bfloat16)
    return pl.pallas_call(
        functools.partial(chip_kernel, count, by_y),
        out_shape=(out,) * count,
        in_specs=[ANYWHERE, ANYWHERE],
        out_specs=(ANYWHERE,) * count,
        scratch_shapes=[held] * 3 + [pltpu.SemaphoreType.DMA((Y * ZH,))] * 3,
        compiler_params=PARAMS,
        cost_estimate=cost(1.9),
        name="chip_sum",
    )(keep, received)


def y_kernel(*refs):
    _, zh, _, _, _ = place_here()
    parts = refs[:Y]
    keep_ref, send_ref, held, keep, send, in_sems, out_sems = refs[Y:]
    arrivals = []
    for j in range(ZH):
        at = zh if j else 1 - zh
        arrivals.append(
            [pltpu.make_async_copy(parts[i].at[at], held.at[j, i], in_sems.at[j, i]) for i in range(Y)]
        )
        for copy in arrivals[j]:
            copy.start()
    out = [
        pltpu.make_async_copy(send, send_ref, out_sems.at[0]),
        pltpu.make_async_copy(keep, keep_ref, out_sems.at[1]),
    ]
    for j in range(ZH):
        for copy in arrivals[j]:
            copy.wait()
        total = sum(held[j, i].astype(jnp.float32) for i in range(Y))
        if j:
            keep[...] = total
        else:
            send[...] = total.astype(jnp.bfloat16)
        out[j].start()
    for copy in out:
        copy.wait()


def y_sum(parts):
    rows = parts[0].shape[1]
    return pl.pallas_call(
        y_kernel,
        out_shape=(
            jax.ShapeDtypeStruct((rows, BLOCK), jnp.float32),
            jax.ShapeDtypeStruct((rows, BLOCK), jnp.bfloat16),
        ),
        in_specs=[ANYWHERE] * Y,
        out_specs=(ANYWHERE, ANYWHERE),
        scratch_shapes=[
            pltpu.VMEM((ZH, Y, rows, BLOCK), jnp.bfloat16),
            pltpu.VMEM((rows, BLOCK), jnp.float32),
            pltpu.VMEM((rows, BLOCK), jnp.bfloat16),
            pltpu.SemaphoreType.DMA((ZH, Y)),
            pltpu.SemaphoreType.DMA((ZH,)),
        ],
        compiler_params=PARAMS,
        cost_estimate=cost(1.8),
        name="y_sum",
    )(*parts)


def apply_kernel(counts, *refs):
    terms = refs[: sum(counts)]
    roots_ref, update_ref, grad_ref = refs[sum(counts) :]
    at = first = 0
    for rows, count in zip(CHUNKS, counts, strict=True):
        grad_ref[at : at + rows] = sum(
            term[...].astype(jnp.float32) for term in terms[first : first + count]
        )
        at += rows
        first += count
    left, right = roots_ref[0].astype(jnp.bfloat16), roots_ref[1].astype(jnp.bfloat16)
    half = mm(grad_ref[...].astype(jnp.bfloat16), right, ((1,), (0,)))
    update_ref[...] = mm(left, half.astype(jnp.bfloat16), ((1,), (0,))).astype(jnp.bfloat16)


def apply_roots(terms, roots):
    counts = [len(group) for group in terms]
    return pl.pallas_call(
        functools.partial(apply_kernel, counts),
        out_shape=(
            jax.ShapeDtypeStruct((BLOCK, BLOCK), jnp.bfloat16),
            jax.ShapeDtypeStruct((BLOCK, BLOCK), jnp.float32),
        ),
        in_specs=[WHOLE] * (sum(counts) + 1),
        out_specs=(WHOLE, WHOLE),
        compiler_params=pltpu.CompilerParams(vmem_limit_bytes=16 * MIB),
        cost_estimate=cost(2.8),
        name="apply_roots",
    )(*[term for group in terms for term in group], roots)


def stats_kernel(grad_ref, stats_ref, out_ref):
    grad = split(grad_ref[...])
    out_ref[0] = 0.95 * stats_ref[0] + mm3(grad, grad, ((1,), (1,)))
    out_ref[1] = 0.95 * stats_ref[1] + mm3(grad, grad, ((0,), (0,)))


def statistics_of(grad, stats):
    return pl.pallas_call(
        stats_kernel,
        out_shape=jax.ShapeDtypeStruct(stats.shape, jnp.float32),
        in_specs=[WHOLE] * 2,
        out_specs=WHOLE,
        compiler_params=PARAMS,
        cost_estimate=cost(3.2),
        name="statistics",
    )(grad, stats)


def roots_kernel(slots, phase, stats_ref, roots_ref, out_ref):
    y, zh, core, _, _ = place_here()
    number = block_in(slots, (y * ZH + zh) * CORE + core)
    refreshed = ((number + phase[0]) & 7) == 0

    @pl.when(jnp.logical_not(refreshed))
    def _():
        out_ref[...] = roots_ref[...]

    @pl.when(refreshed)
    def _():
        row = lax.broadcasted_iota(jnp.int32, (BLOCK, BLOCK), 0)
        col = lax.broadcasted_iota(jnp.int32, (BLOCK, BLOCK), 1)
        identity = (row == col).astype(jnp.float32)

        def times(a, b):
            return mm(a.astype(jnp.bfloat16), b.astype(jnp.bfloat16), ((1,), (0,)))

        def powered(coupled):
            rest = times(coupled, coupled) * 0.0625 - 0.625 * coupled
            rest = times(rest, rest) + 3.125 * rest
            return times(rest, coupled) + 2.44140625 * coupled

        for side in range(2):
            matrix = stats_ref[side]
            scaling = 2.5 / jnp.sqrt(jnp.sum(matrix * matrix, keepdims=True))
            first = matrix * scaling
            second = powered(first)
            third = powered(second)
            both = times(first, second) * 0.0625 - 0.3125 * (first + second) + 1.5625 * identity
            found = 1.25 * both - 0.25 * times(both, third)
            out_ref[side] = found * jnp.sqrt(jnp.sqrt(scaling))


def roots_of(slot_of, phase, stats, roots):
    return pl.pallas_call(
        roots_kernel,
        out_shape=jax.ShapeDtypeStruct(stats.shape, jnp.float32),
        in_specs=[SCALARS, SCALARS, WHOLE, WHOLE],
        out_specs=WHOLE,
        compiler_params=PARAMS,
        cost_estimate=cost(4.0),
        name="roots",
    )(slot_of, phase, stats, roots)


def place_kernel(whence, aliased, slots, *refs):
    y, zh, core, _, _ = place_here()
    count = len(whence)
    blocks = refs[:count]
    out_ref, held, in_sems, out_sems = refs[count + aliased :]
    arrivals = [
        pltpu.make_async_copy(blocks[i], held.at[i], in_sems.at[i]) for i in range(count)
    ]
    for copy in arrivals:
        copy.start()
    copies = []
    for i in range(count):
        hop, other_z, other_core = whence[i]
        there = 1 - core if other_core else core
        at_z = 1 - zh if other_z else zh
        number = block_in(slots, (((y + hops(there)[hop]) & 3) * ZH + at_z) * CORE + there)
        row = pl.multiple_of(number // COL_BLK * BLOCK, BLOCK)
        col = pl.multiple_of(number % COL_BLK * BLOCK, BLOCK)
        arrivals[i].wait()
        copy = pltpu.make_async_copy(
            held.at[i], out_ref.at[pl.ds(row, BLOCK), pl.ds(col, BLOCK)], out_sems.at[i]
        )
        copy.start()
        copies.append(copy)
    for copy in copies:
        copy.wait()


def place(found, slot_of, into, cols):
    blocks, whence = [entry[0] for entry in found], [entry[1:] for entry in found]
    count = len(found)
    aliased = into is not None
    return pl.pallas_call(
        functools.partial(place_kernel, whence, int(aliased)),
        out_shape=jax.ShapeDtypeStruct((FEAT, cols), jnp.bfloat16),
        in_specs=[SCALARS] + [ANYWHERE] * (count + aliased),
        out_specs=ANYWHERE,
        scratch_shapes=[
            pltpu.VMEM((count, BLOCK, BLOCK), jnp.bfloat16),
            pltpu.SemaphoreType.DMA((count,)),
            pltpu.SemaphoreType.DMA((count,)),
        ],
        input_output_aliases={count + 1: 0} if aliased else {},
        compiler_params=PARAMS,
        cost_estimate=cost(3.7),
        name="place",
    )(slot_of, *blocks, *([into] if aliased else []))


def after(value, *others):
    return lax.optimization_barrier((value, *others))[0]


def body(activations, out_grad, statistics, root_blocks, owner_slots, stagger_phase):
    slot_of = owner_slots[0]
    roots = root_blocks[0, 0]
    tokens = activations.shape[0]
    cols = out_grad.shape[1]
    by_block = activations.reshape(tokens, ROW_BLK, BLOCK)
    owns = []
    at = 0
    for rows in CHUNKS:
        owns.append(by_block[:, :, at : at + rows].transpose(1, 2, 0).reshape(ROW_BLK * rows, tokens))
        at += rows

    far_a, across_a = move(owns[0], X_FAR), move(owns[0], ZL_SWAP)
    near_a, back_a = move(owns[0], X_NEAR), move(owns[0], X_BACK)
    across_b = move(after(owns[1], across_a), ZL_SWAP)
    rest_a = [move(across_a, X_NEAR), move(across_a, X_BACK), move(far_a, ZL_SWAP)]
    own_b = after(owns[1], far_a)
    near_b, back_b = move(own_b, X_NEAR), move(own_b, X_BACK)

    pieces = [owns[0], near_a, back_a, far_a, across_a, *rest_a]
    keep_a, send_a = grad_chunk(pieces, slot_of, out_grad, CHUNKS[0])
    swapped_a = move(after(send_a, near_b, back_b, across_b), C_SWAP)
    across_b = after(across_b, keep_a)
    far_b = move(after(near_b, keep_a), X_NEAR)
    mine, *to = chip_sum(keep_a, swapped_a, True)
    rest_b = [move(across_b, X_NEAR), move(across_b, X_BACK), move(after(far_b, mine), ZL_SWAP)]
    parts = [mine, move(to[0], Y_NEAR), move(to[1], Y_BACK), move(to[2], Y_FAR)]

    rest_b[0] = after(rest_b[0], parts[1], parts[2])
    pieces = [owns[1], near_b, back_b, far_b, across_b, *rest_b]
    keep_b, send_b = grad_chunk(pieces, slot_of, out_grad, CHUNKS[1])
    swapped_b = move(after(send_b, *parts[1:]), C_SWAP)
    keep_a, send_a = y_sum(parts)
    mine, *to = chip_sum(keep_b, after(swapped_b, send_a), False)
    to = [part[0] for part in to]
    near, back, far = move(to[0], Y_NEAR), move(to[1], Y_BACK), move(to[2], Y_FAR)
    terms_b = [mine[0], near, back, far, move(to[3], ZH_SWAP), move(to[6], Y_FAR_Z)]
    terms_b += [move(to[4], Y_NEAR_Z), move(to[5], Y_BACK_Z)]
    terms_a = [keep_a, move(send_a, ZH_SWAP)]

    own, grad = apply_roots([terms_a, terms_b], roots)

    across, near, back = move(own, ZH_SWAP), move(own, Y_NEAR), move(own, Y_BACK)
    own_other = move(own, C_SWAP)
    new_stats = statistics_of(grad, statistics[0, 0])
    near = after(near, new_stats, own_other)
    far = move(near, Y_NEAR)
    across, far_ = after(across, far), after(far, back)
    across_near, across_back = move(across, Y_NEAR), move(across, Y_BACK)
    across_far = move(far_, ZH_SWAP)
    new_roots = roots_of(slot_of, stagger_phase, after(new_stats, far), roots)
    found = [(own, 0, False, False), (own_other, 0, False, True)]
    found += [(near, 1, False, False), (move(near, C_SWAP), 1, False, True)]
    found += [(back, 2, False, False), (move(back, C_SWAP), 2, False, True)]
    found += [(across, 0, True, False), (far, 3, False, False)]
    update = place(found, slot_of, None, cols)

    found = []
    for block, hop in ((across_near, 1), (across_back, 2), (across_far, 3)):
        block = after(block, update, new_roots)
        found += [(block, hop, True, False), (move(block, C_SWAP), hop, True, True)]
    found.append((move(after(across, update, new_roots), C_SWAP), 0, True, True))
    found.append((move(after(far, update, new_roots), C_SWAP), 3, False, True))
    update = place(found, slot_of, update, cols)
    return (update, new_stats[None, None], new_roots[None, None])


def solution(mesh):
    return jax.shard_map(
        body,
        mesh=mesh,
        in_specs=(
            P(("dp", "mp"), None),
            P("dp", "mp"),
            P("mp", "dp", None, None, None),
            P("mp", "dp", None, None, None),
            P("mp", None),
            P("mp"),
        ),
        out_specs=(P(None, "mp"), P("mp", "dp", None, None, None), P("mp", "dp", None, None, None)),
        check_vma=False,
    )
```
